512 devices in a mesh: row: 32 (over x, y, core), col: 16 (over z).
Axes of the slice: x: 4, y: 4, z: 16, core: 2. Of those that a mesh axis runs over, the one named last changes fastest.
Arguments:
- left_blocks: float32 [2, 32, 32, 128, 128], P(None, 'row', 'col'), may hold values from -6 to 6
- left_index: int32 [2, 2, 32, 32], P(None, None, 'row', 'col'), may hold values from -1 to 31, as said below
- right_blocks: float32 [2, 32, 16, 128, 128], P(None, 'row', 'col'), may hold values from -0.5 to 0.5
- right_index: int32 [2, 2, 32, 16], P(None, None, 'row', 'col'), may hold values from -1 to 31, as said below
Outputs:
- product: float32 [16384, 8192], P('row', 'col')
The draws below stay inside these ranges and needn't reach their ends.
Inputs may be any that keep to these rules, and one draw needn't show every extreme that they name: left_index[s, 0, r, t] is the block row within the band of 4 block rows, or -1 for an empty slot whose block is not used. left_index[s, 1, r, t] is a block column of the panel; slot t belongs to index t // 2 of col, which stores only the 32 / 16 block columns from (t // 2) * 32 / 16 on. The live slots of one device in one step name distinct blocks; in every step some device has all 2 slots live. right_index[s, 0, q, c] is a block row of the panel, or -1 for an empty slot whose block is not used; slot q belongs to index q // 1 of row, which stores only the 32 / 32 block rows from (q // 1) * 32 / 32 on. right_index[s, 1, q, c] is the block column within the band of 4. The live slots of one device in one step name distinct blocks; in every step some device has all 1 slots live.
All inputs are finite; a program needn't handle non-finite values.
Results may differ from the reference program's by a relative error of at most 0.0003.
Values sent between devices are 32-bit elements; how exact they have to be, the bound alone decides.
No kernel may reach another device: no remote copies, remote signals or barrier semaphores. Data moves between devices by JAX's collectives and lax.ppermute only.
A program may use at most 64 MiB of HBM per device.

```python
import jax
import jax.numpy as jnp
from jax import lax

BS = 128
PANEL = 32
STEPS = 2
BR = 4
BC = 4
LCAP = 2
RCAP = 1
N_ROW = 32
N_COL = 16


def pick_slots(key, pieces, candidates, capacity):
    subkeys = jax.random.split(key, pieces + 2)
    orders = jax.vmap(lambda subkey: jax.random.permutation(subkey, candidates))(subkeys[:pieces])
    chosen = orders[:, :capacity].astype(jnp.int32)
    counts = jax.random.randint(subkeys[pieces], (pieces,), 0, capacity + 1)
    fullest = jax.random.randint(subkeys[pieces + 1], (), 0, pieces)
    counts = jnp.where(jnp.arange(pieces) == fullest, capacity, counts)
    active = jnp.arange(capacity)[None, :] < counts[:, None]
    return (chosen, active)


def draw_left_index(key, part):
    cols_owned = PANEL // N_COL
    planes = []
    for section in range(STEPS):
        chosen, active = pick_slots(jax.random.fold_in(key, 101 + section), N_ROW * N_COL, BR * cols_owned, LCAP)
        owners = (jnp.arange(N_ROW * N_COL) % N_COL).astype(jnp.int32)
        block_row = jnp.where(active, chosen // cols_owned, -1)
        block_col = chosen % cols_owned + owners[:, None] * cols_owned
        planes.append(jnp.stack([block_row.reshape(N_ROW, N_COL * LCAP), block_col.reshape(N_ROW, N_COL * LCAP)]))
    return jnp.stack(planes).astype(jnp.int32)


def draw_right_index(key, part):
    rows_owned = PANEL // N_ROW
    planes = []
    for section in range(STEPS):
        chosen, active = pick_slots(jax.random.fold_in(key, 202 + section), N_ROW * N_COL, rows_owned * BC, RCAP)
        owners = (jnp.arange(N_ROW * N_COL) // N_COL).astype(jnp.int32)
        block_row = jnp.where(active, chosen // BC + owners[:, None] * rows_owned, -1)
        block_col = chosen % BC
        block_row = block_row.reshape(N_ROW, N_COL, RCAP).transpose(0, 2, 1).reshape(N_ROW * RCAP, N_COL)
        block_col = block_col.reshape(N_ROW, N_COL, RCAP).transpose(0, 2, 1).reshape(N_ROW * RCAP, N_COL)
        planes.append(jnp.stack([block_row, block_col]))
    return jnp.stack(planes).astype(jnp.int32)


def shard_levels(own_key, shape, cuts, smallest, top_value):
    factor_of, own = 1.0, jax.random.fold_in(own_key, 6)
    for position, parts in cuts:
        steps = jnp.exp(jax.random.uniform(jax.random.fold_in(own, position), (parts,), jnp.float32, smallest / len(cuts), top_value / len(cuts)))
        factor_of = factor_of * jnp.repeat(steps, shape[position] // parts).reshape([-1 if axis == position else 1 for axis in range(len(shape))])
    return factor_of


def noise(stream_key, extent, scale, limit, shards=(), held_as=jnp.bfloat16):
    values = jax.random.normal(stream_key, extent, jnp.float32) * scale
    if len(shards) > 0:
        values = shard_levels(stream_key, extent, shards, -0.22, 0.18) * values
    return jnp.clip(values, min=-limit, max=limit).astype(held_as)


def setup_inputs(seed: int = 0) -> dict:
    seeds = jax.random.split(jax.random.key(seed), 5)
    return {
        "left_blocks": noise(seeds[0], (STEPS, N_ROW, N_COL * LCAP, BS, BS), 1.0, 6.0, ((1, 32), (2, 16)), jnp.float32),
        "left_index": draw_left_index(jax.random.fold_in(seeds[4], 71), 0),
        "right_blocks": noise(seeds[2], (STEPS, N_ROW * RCAP, N_COL, BS, BS), BS ** -0.5, 0.5, ((1, 32), (2, 16)), jnp.float32),
        "right_index": draw_right_index(jax.random.fold_in(seeds[4], 71), 0),
    }


precise_mode = lax.Precision.HIGHEST


def panel_product(left_part, left_where, right_part, right_where, capacity, owned_rows, row_span, col_span):
    left_rows = left_where[0]
    left_cols = left_where[1]
    owners = left_cols // owned_rows
    picked = owners[:, None] * capacity + jnp.arange(capacity, dtype=jnp.int32)[None, :]
    right_pick = right_part[picked]
    right_rows = right_where[0][picked]
    right_cols = right_where[1][picked]
    matched = (right_rows == left_cols[:, None]) & (left_rows[:, None] >= 0)
    products = jnp.einsum("lab,lqbc->lqac", left_part, right_pick, precision=precise_mode)
    target = left_rows[:, None] * col_span + right_cols
    slots_out = jnp.arange(row_span * col_span, dtype=jnp.int32)
    placing = ((target[:, :, None] == slots_out[None, None, :]) & matched[:, :, None]).astype(jnp.float32)
    summed = jnp.einsum("lqac,lqn->nac", products, placing, precision=precise_mode)
    block_size = left_part.shape[1]
    summed = summed.reshape(row_span, col_span, block_size, block_size)
    return summed.transpose(0, 2, 1, 3).reshape(row_span * block_size, col_span * block_size)


def reference(left_blocks, left_index, right_blocks, right_index):
    owned_rows = PANEL // N_ROW

    def one_band(band_index):
        running_sum = jnp.zeros((N_COL, BR * BS, BC * BS), jnp.float32)
        for section in range(STEPS):
            left_part = left_blocks[section, band_index]
            left_where = left_index[section, :, band_index]

            def per_column(right_part, right_where):
                return panel_product(left_part, left_where, right_part, right_where, RCAP, owned_rows, BR, BC)

            running_sum = running_sum + jax.vmap(per_column, in_axes=(1, 2))(right_blocks[section], right_index[section])
        return running_sum

    bands = lax.map(one_band, jnp.arange(N_ROW, dtype=jnp.int32))
    return bands.transpose(0, 2, 1, 3).reshape(N_ROW * BR * BS, N_COL * BC * BS)
```

```python
import jax
import jax.numpy as jnp
from jax import lax
from jax.experimental import pallas as pl
from jax.experimental.pallas import tpu as pltpu
from jax.sharding import PartitionSpec as P

BS = 128
STEPS = 2
BR = 4
BC = 4
LCAP = 2
N_ROW = 32
N_COL = 16
SLOTS = STEPS * LCAP
UNROLL = 4
F32 = jnp.float32


def along_col(x, step):
    return lax.ppermute(x, "col", [(z, (z + step) % N_COL) for z in range(N_COL)])


def packed(blocks, index):
    where = index.reshape(1, -1).astype(F32)
    where = jnp.pad(where, ((0, 7), (0, BS - where.shape[1])))
    return jnp.concatenate([blocks.reshape(-1, BS), where], axis=0)


def split(x):
    high = x.astype(jnp.bfloat16)
    return high, (x - high.astype(F32)).astype(jnp.bfloat16)


def product_kernel(right, *refs):
    lefts, out_ref = refs[:N_COL], refs[N_COL]
    l_buf, r_buf, l_where, r_where, todo, acc, where_sem, sem = refs[N_COL + 1 :]
    tile = pl.ds(SLOTS * BS, 8)
    wheres = [pltpu.make_async_copy(right.at[:, pl.ds(STEPS * BS, 8)], r_where, where_sem.at[N_COL])]
    blocks = [pltpu.make_async_copy(right, r_buf, sem.at[N_COL])]
    for u, left in enumerate(lefts):
        wheres.append(pltpu.make_async_copy(left.at[tile], l_where.at[u], where_sem.at[u]))
        blocks.append(pltpu.make_async_copy(left, l_buf.at[u], sem.at[u]))
    for copy in wheres + blocks:
        copy.start()
    acc[...] = jnp.zeros_like(acc)
    for copy in wheres:
        copy.wait()

    def look(u, count):
        for s in range(STEPS):
            for t in range(LCAP):
                i = l_where[u, 0, s * 2 * LCAP + t].astype(jnp.int32)
                k = l_where[u, 0, s * 2 * LCAP + LCAP + t].astype(jnp.int32)
                k = jnp.clip(k, 0, N_ROW - 1)
                row = r_where[k, 0, s * 2].astype(jnp.int32)
                j = r_where[k, 0, s * 2 + 1].astype(jnp.int32)
                todo[0, count] = u
                todo[1, count] = (s * LCAP + t) * BS
                todo[2, count] = k
                todo[3, count] = s * BS
                todo[4, count] = i * BC + j
                count = count + ((i >= 0) & (row == k)).astype(jnp.int32)
        return count

    count = lax.fori_loop(0, N_COL, look, jnp.int32(0))
    for n in range(UNROLL - 1):
        for field in range(4):
            todo[field, count + n] = 0
        todo[4, count + n] = BR * BC
    for copy in blocks:
        copy.wait()

    def multiply(step, carry):
        sums = []
        for n in range(UNROLL):
            at = step * UNROLL + n
            a = l_buf[todo[0, at], pl.ds(pl.multiple_of(todo[1, at], BS), BS), :]
            b = r_buf[todo[2, at], pl.ds(pl.multiple_of(todo[3, at], BS), BS), :]
            a = jnp.concatenate(split(a), axis=1)
            b = jnp.concatenate(split(b), axis=1)
            both = jnp.dot(a, jnp.concatenate([b, b], axis=0), preferred_element_type=F32)
            sums.append(both[:, :BS] + both[:, BS:])
        for n in range(UNROLL):
            acc[todo[4, step * UNROLL + n]] += sums[n]
        return carry

    lax.fori_loop(0, (count + UNROLL - 1) // UNROLL, multiply, 0)
    for i in range(BR):
        for j in range(BC):
            out_ref[pl.ds(i * BS, BS), pl.ds(j * BS, BS)] = acc[i * BC + j]


def products(lefts, right):
    most = N_COL * SLOTS + UNROLL
    hbm = pl.BlockSpec(memory_space=pltpu.HBM)
    return pl.pallas_call(
        product_kernel,
        out_shape=jax.ShapeDtypeStruct((BR * BS, BC * BS), F32),
        in_specs=[hbm] * (N_COL + 1),
        out_specs=pl.BlockSpec(memory_space=pltpu.VMEM),
        scratch_shapes=[
            pltpu.VMEM((N_COL,) + lefts[0].shape, F32),
            pltpu.VMEM(right.shape, F32),
            pltpu.SMEM((N_COL, 8, BS), F32),
            pltpu.SMEM((N_ROW, 8, BS), F32),
            pltpu.SMEM((5, most), jnp.int32),
            pltpu.VMEM((BR * BC + 1, BS, BS), F32),
            pltpu.SemaphoreType.DMA((N_COL + 1,)),
            pltpu.SemaphoreType.DMA((N_COL + 1,)),
        ],
        compiler_params=pltpu.CompilerParams(vmem_limit_bytes=48 * 1024 * 1024),
    )(right, *lefts)


def per_device(left_blocks, left_index, right_blocks, right_index):
    own = packed(left_blocks, left_index)
    right = lax.all_gather(packed(right_blocks, right_index), "row", axis=0)
    lefts, up, down = [own], own, own
    for hop in range(1, N_COL // 2 + 1):
        up = along_col(up, 1)
        lefts.append(up)
        if hop < N_COL // 2:
            down = along_col(down, -1)
            lefts.append(down)
    return products(lefts, right)


def solution(mesh):
    placed = (
        P(None, "row", "col", None, None),
        P(None, None, "row", "col"),
        P(None, "row", "col", None, None),
        P(None, None, "row", "col"),
    )
    return jax.shard_map(
        per_device, mesh=mesh, in_specs=placed, out_specs=P("row", "col"), check_vma=False
    )
```

```python
import jax
import jax.numpy as jnp
from jax import lax
from jax.experimental import pallas as pl
from jax.experimental.pallas import tpu as pltpu
from jax.sharding import PartitionSpec as P

BS = 128
STEPS = 2
BR = 4
BC = 4
LCAP = 2
N_ROW = 32
N_COL = 16
SIDE = 4
AREA = SIDE * SIDE
SLOTS = STEPS * LCAP
UNROLL = 4
PARTS = 4
MOST = N_COL * SLOTS
F32 = jnp.float32
I32 = jnp.int32


def along_row(x, dx, dy, dc):
    pairs = []
    for r in range(N_ROW):
        a, b, c = r // (2 * SIDE), r // 2 % SIDE, r % 2
        to = ((a + dx) % SIDE * SIDE + (b + dy) % SIDE) * 2 + (c ^ dc)
        pairs.append((r, to))
    return lax.ppermute(x, "row", pairs)


def packed(blocks, index):
    where = index.reshape(1, -1).astype(F32)
    where = jnp.pad(where, ((0, 7), (0, BS - where.shape[1])))
    return jnp.concatenate([blocks.reshape(-1, BS), where], axis=0)


def split(x):
    high = x.astype(jnp.bfloat16)
    return high, (x - high.astype(F32)).astype(jnp.bfloat16)


def match_kernel(me, l_where, mine, other, todo, r_where, sem):
    copies = [
        pltpu.make_async_copy(ref.at[:, pl.ds(STEPS * BS, 8)], r_where.at[h], sem.at[h])
        for h, ref in enumerate((mine, other))
    ]
    for copy in copies:
        copy.start()
    for copy in copies:
        copy.wait()

    def look(u, count):
        for s in range(STEPS):
            for t in range(LCAP):
                i = l_where[u * 2 * SLOTS + s * 2 * LCAP + t]
                k = jnp.clip(l_where[u * 2 * SLOTS + s * 2 * LCAP + LCAP + t], 0, N_ROW - 1)
                dx = (me[0] + SIDE - lax.shift_right_logical(k, 3)) & (SIDE - 1)
                dy = (me[1] + SIDE - (lax.shift_right_logical(k, 1) & (SIDE - 1))) & (SIDE - 1)
                half = (me[2] + k) & 1
                place = dy * SIDE + dx
                row = r_where[half, place, 0, s * 2].astype(I32)
                j = r_where[half, place, 0, s * 2 + 1].astype(I32)
                todo[0, count] = u
                todo[1, count] = (s * LCAP + t) * BS
                todo[2, count] = half * AREA + place
                todo[3, count] = s * BS
                todo[4, count] = i * BC + j
                count = count + ((i >= 0) & (row == k)).astype(I32)
        return count

    count = lax.fori_loop(0, N_COL, look, jnp.int32(0))
    for n in range(UNROLL - 1):
        for field in range(4):
            todo[field, count + n] = 0
        todo[4, count + n] = BR * BC
    todo[5, 0] = count


def product_kernel(todo, left, mine, other, out_ref, l_buf, r_buf, acc, l_sem, r_sem):
    count = todo[5, 0]
    rights = [
        pltpu.make_async_copy(ref, r_buf.at[pl.ds(h * AREA, AREA)], r_sem.at[h])
        for h, ref in enumerate((mine, other))
    ]
    lefts = [
        pltpu.make_async_copy(left.at[part], l_buf.at[part], l_sem.at[n])
        for n, part in enumerate(pl.ds(u, N_COL // PARTS) for u in range(0, N_COL, N_COL // PARTS))
    ]
    for copy in lefts + rights:
        copy.start()
    steps = lax.div(count + UNROLL - 1, UNROLL)
    acc[...] = jnp.zeros_like(acc)
    for copy in lefts + rights:
        copy.wait()

    def multiply(step, carry):
        sums = []
        for n in range(UNROLL):
            at = step * UNROLL + n
            a = l_buf[todo[0, at], pl.ds(pl.multiple_of(todo[1, at], BS), BS), :]
            b = r_buf[todo[2, at], pl.ds(pl.multiple_of(todo[3, at], BS), BS), :]
            a = jnp.concatenate(split(a), axis=1)
            b = jnp.concatenate(split(b), axis=1)
            both = jnp.dot(a, jnp.concatenate([b, b], axis=0), preferred_element_type=F32)
            sums.append(both[:, :BS] + both[:, BS:])
        for n in range(UNROLL):
            acc[todo[4, step * UNROLL + n]] += sums[n]
        return carry

    lax.fori_loop(0, steps, multiply, 0)
    for i in range(BR):
        for j in range(BC):
            out_ref[pl.ds(i * BS, BS), pl.ds(j * BS, BS)] = acc[i * BC + j]


HBM = pl.BlockSpec(memory_space=pltpu.HBM)
SMEM = pl.BlockSpec(memory_space=pltpu.SMEM)


def matches(me, l_where, mine, other):
    return pl.pallas_call(
        match_kernel,
        out_shape=jax.ShapeDtypeStruct((6, MOST + UNROLL), I32),
        in_specs=[SMEM, SMEM, HBM, HBM],
        out_specs=SMEM,
        scratch_shapes=[pltpu.SMEM((2, AREA, 8, BS), F32), pltpu.SemaphoreType.DMA((2,))],
        compiler_params=pltpu.CompilerParams(vmem_limit_bytes=60 * 1024 * 1024),
    )(me, l_where, mine, other)


def products(todo, left, mine, other):
    return pl.pallas_call(
        product_kernel,
        out_shape=jax.ShapeDtypeStruct((BR * BS, BC * BS), F32),
        in_specs=[SMEM, HBM, HBM, HBM],
        out_specs=pl.BlockSpec(memory_space=pltpu.VMEM),
        scratch_shapes=[
            pltpu.VMEM(left.shape, F32),
            pltpu.VMEM((2 * AREA,) + mine.shape[1:], F32),
            pltpu.VMEM((BR * BC + 1, BS, BS), F32),
            pltpu.SemaphoreType.DMA((PARTS,)),
            pltpu.SemaphoreType.DMA((2,)),
        ],
        compiler_params=pltpu.CompilerParams(vmem_limit_bytes=60 * 1024 * 1024),
    )(todo, left, mine, other)


def per_device(left_blocks, left_index, right_blocks, right_index):
    left = lax.all_gather(left_blocks.reshape(SLOTS * BS, BS), "col", axis=0)
    mine = packed(right_blocks, right_index)
    line = jnp.stack([mine, *[along_row(mine, d, 0, 0) for d in (1, 2, 3)]])
    l_index, line = lax.optimization_barrier((left_index, line))
    l_where = lax.all_gather(l_index.reshape(-1), "col", axis=0, tiled=True)
    area = jnp.concatenate([line, *[along_row(line, 0, d, 0) for d in (1, 2, 3)]])
    area, l_where = lax.optimization_barrier((area, l_where))
    other = along_row(area, 0, 0, 1)
    row = lax.axis_index("row")
    me = jnp.stack([row // (2 * SIDE), row // 2 % SIDE, row % 2]).astype(I32)
    todo = matches(me, l_where, area, other)
    return products(todo, left, area, other)


def solution(mesh):
    placed = (
        P(None, "row", "col", None, None),
        P(None, None, "row", "col"),
        P(None, "row", "col", None, None),
        P(None, None, "row", "col"),
    )
    return jax.shard_map(
        per_device, mesh=mesh, in_specs=placed, out_specs=P("row", "col"), check_vma=False
    )
```

```python
import jax
import jax.numpy as jnp
from jax import lax
from jax.experimental import pallas as pl
from jax.experimental.pallas import tpu as pltpu
from jax.sharding import PartitionSpec as P

BS = 128
STEPS = 2
BR = 4
BC = 4
LCAP = 2
N_ROW = 32
N_COL = 16
SIDE = 4
AREA = SIDE * SIDE
SLOTS = STEPS * LCAP
UNROLL = 4
LIMIT = 60
MOST = N_COL * SLOTS
F32 = jnp.float32
I32 = jnp.int32


def along_row(x, dx, dy, dc):
    pairs = []
    for r in range(N_ROW):
        a, b, c = r // (2 * SIDE), r // 2 % SIDE, r % 2
        to = ((a + dx) % SIDE * SIDE + (b + dy) % SIDE) * 2 + (c ^ dc)
        pairs.append((r, to))
    return lax.ppermute(x, "row", pairs)


def packed(blocks, index):
    where = index.reshape(1, -1).astype(F32)
    where = jnp.pad(where, ((0, 7), (0, BS - where.shape[1])))
    return jnp.concatenate([blocks.reshape(-1, BS), where], axis=0)


def split(x):
    high = x.astype(jnp.bfloat16)
    return high, (x - high.astype(F32)).astype(jnp.bfloat16)


def match_kernel(me, l_where, mine, other, todo, staged, r_buf, r_where, sem):
    copies = []
    for h, ref in enumerate((mine, other)):
        tile = ref.at[:, pl.ds(STEPS * BS, 8)]
        copies.append(pltpu.make_async_copy(tile, r_where.at[h], sem.at[h]))
    for h, ref in enumerate((mine, other)):
        half = r_buf.at[pl.ds(h * AREA, AREA)]
        copies.append(pltpu.make_async_copy(ref, half, sem.at[2 + h]))
    for copy in copies:
        copy.start()
    copies[0].wait()
    copies[1].wait()

    def look(u, count):
        for s in range(STEPS):
            for t in range(LCAP):
                i = l_where[u * 2 * SLOTS + s * 2 * LCAP + t]
                k = jnp.clip(l_where[u * 2 * SLOTS + s * 2 * LCAP + LCAP + t], 0, N_ROW - 1)
                dx = (me[0] + SIDE - lax.shift_right_logical(k, 3)) & (SIDE - 1)
                dy = (me[1] + SIDE - (lax.shift_right_logical(k, 1) & (SIDE - 1))) & (SIDE - 1)
                half = (me[2] + k) & 1
                place = dy * SIDE + dx
                row = r_where[half, place, 0, s * 2].astype(I32)
                j = r_where[half, place, 0, s * 2 + 1].astype(I32)
                todo[0, count] = u
                todo[1, count] = (s * LCAP + t) * BS
                todo[2, count] = half * AREA + place
                todo[3, count] = s * BS
                todo[4, count] = i * BC + j
                count = count + ((i >= 0) & (row == k)).astype(I32)
        return count

    count = lax.fori_loop(0, N_COL, look, jnp.int32(0))
    copies[2].wait()
    copies[3].wait()

    def stage(n, carry):
        rows = pl.ds(pl.multiple_of(todo[3, n], BS), BS)
        staged[n] = jnp.concatenate(split(r_buf[todo[2, n], rows, :]), axis=1)
        return carry

    lax.fori_loop(0, count, stage, 0)
    for n in range(UNROLL - 1):
        staged[count + n] = jnp.zeros(staged.shape[1:], staged.dtype)
        for field in range(5):
            todo[field, count + n] = 0
    todo[5, 0] = count


def product_kernel(todo, left, staged, out_ref, l_buf, r_buf, sem, r_sem):
    steps = lax.div(todo[5, 0] + UNROLL - 1, UNROLL)

    def fetch(n):
        rows = pl.ds(pl.multiple_of(todo[1, n], BS), BS)
        return pltpu.make_async_copy(left.at[todo[0, n], rows], l_buf.at[n], sem.at[n])

    def fetch_staged(step):
        some = pl.ds(step * UNROLL, UNROLL)
        return pltpu.make_async_copy(staged.at[some], r_buf.at[some], r_sem.at[step])

    def start(step, carry):
        for n in range(UNROLL):
            fetch(step * UNROLL + n).start()
        fetch_staged(step).start()
        return carry

    lax.fori_loop(0, steps, start, 0)
    out_ref[...] = jnp.zeros_like(out_ref)

    def multiply(step, carry):
        for n in range(UNROLL):
            fetch(step * UNROLL + n).wait()
        fetch_staged(step).wait()
        sums = []
        for n in range(UNROLL):
            at = step * UNROLL + n
            a = jnp.concatenate(split(l_buf[at]), axis=1)
            b = r_buf[at]
            both = jnp.dot(a, jnp.concatenate([b, b], axis=0), preferred_element_type=F32)
            sums.append(both[:, :BS] + both[:, BS:])
        for n in range(UNROLL):
            at = todo[4, step * UNROLL + n]
            rows = pl.ds(pl.multiple_of(lax.shift_right_logical(at, 2) * BS, BS), BS)
            cols = pl.ds(pl.multiple_of((at & (BC - 1)) * BS, BS), BS)
            out_ref[rows, cols] += sums[n]
        return carry

    lax.fori_loop(0, steps, multiply, 0)


HBM = pl.BlockSpec(memory_space=pltpu.HBM)
SMEM = pl.BlockSpec(memory_space=pltpu.SMEM)


VMEM = pl.BlockSpec(memory_space=pltpu.VMEM)
ROOM = pltpu.CompilerParams(vmem_limit_bytes=LIMIT * 1024 * 1024)


def matches(me, l_where, mine, other):
    return pl.pallas_call(
        match_kernel,
        out_shape=[
            jax.ShapeDtypeStruct((6, MOST + UNROLL), I32),
            jax.ShapeDtypeStruct((MOST + UNROLL, BS, 2 * BS), jnp.bfloat16),
        ],
        in_specs=[SMEM, SMEM, HBM, HBM],
        out_specs=[SMEM, VMEM],
        scratch_shapes=[
            pltpu.VMEM((2 * AREA,) + mine.shape[1:], F32),
            pltpu.SMEM((2, AREA, 8, BS), F32),
            pltpu.SemaphoreType.DMA((4,)),
        ],
        compiler_params=ROOM,
    )(me, l_where, mine, other)


def products(todo, left, staged):
    return pl.pallas_call(
        product_kernel,
        out_shape=jax.ShapeDtypeStruct((BR * BS, BC * BS), F32),
        in_specs=[SMEM, HBM, HBM],
        out_specs=VMEM,
        scratch_shapes=[
            pltpu.VMEM((MOST + UNROLL, BS, BS), F32),
            pltpu.VMEM(staged.shape, staged.dtype),
            pltpu.SemaphoreType.DMA((MOST + UNROLL,)),
            pltpu.SemaphoreType.DMA((MOST // UNROLL,)),
        ],
        compiler_params=ROOM,
    )(todo, left, staged)


def per_device(left_blocks, left_index, right_blocks, right_index):
    left = lax.all_gather(left_blocks.reshape(SLOTS * BS, BS), "col", axis=0)
    mine = packed(right_blocks, right_index)
    line = jnp.stack([mine, *[along_row(mine, d, 0, 0) for d in (1, 2, 3)]])
    l_index, line = lax.optimization_barrier((left_index, line))
    l_where = lax.all_gather(l_index.reshape(-1), "col", axis=0, tiled=True)
    area = jnp.concatenate([line, *[along_row(line, 0, d, 0) for d in (1, 2, 3)]])
    area, l_where = lax.optimization_barrier((area, l_where))
    other = along_row(area, 0, 0, 1)
    row = lax.axis_index("row")
    me = jnp.stack([row // (2 * SIDE), row // 2 % SIDE, row % 2]).astype(I32)
    todo, staged = matches(me, l_where, area, other)
    return products(todo, left, staged)


def solution(mesh):
    placed = (
        P(None, "row", "col", None, None),
        P(None, None, "row", "col"),
        P(None, "row", "col", None, None),
        P(None, None, "row", "col"),
    )
    return jax.shard_map(
        per_device, mesh=mesh, in_specs=placed, out_specs=P("row", "col"), check_vma=False
    )
```

```python
import jax
import jax.numpy as jnp
from jax import lax
from jax.experimental import pallas as pl
from jax.experimental.pallas import tpu as pltpu
from jax.sharding import PartitionSpec as P

BS = 128
STEPS = 2
BR = 4
BC = 4
LCAP = 2
N_ROW = 32
N_COL = 16
SIDE = 4
AREA = SIDE * SIDE
SLOTS = STEPS * LCAP
UNROLL = 4
REST = 112
MAIN = SLOTS * BS - REST
LIMIT = 60
MOST = N_COL * SLOTS
F32 = jnp.float32
I32 = jnp.int32


def along_row(x, dx, dy, dc):
    pairs = []
    for r in range(N_ROW):
        a, b, c = r // (2 * SIDE), r // 2 % SIDE, r % 2
        to = ((a + dx) % SIDE * SIDE + (b + dy) % SIDE) * 2 + (c ^ dc)
        pairs.append((r, to))
    return lax.ppermute(x, "row", pairs)


def packed(blocks, index):
    where = index.reshape(1, -1).astype(F32)
    where = jnp.pad(where, ((0, 7), (0, BS - where.shape[1])))
    return jnp.concatenate([blocks.reshape(-1, BS), where], axis=0)


def split(x):
    high = x.astype(jnp.bfloat16)
    return high, (x - high.astype(F32)).astype(jnp.bfloat16)


def match_kernel(me, rest, mine, other, todo, staged, r_buf, l_where, r_where, sem):
    copies = [pltpu.make_async_copy(rest.at[:, pl.ds(REST, 8)], l_where, sem.at[4])]
    for h, ref in enumerate((mine, other)):
        tile = ref.at[:, pl.ds(STEPS * BS, 8)]
        copies.append(pltpu.make_async_copy(tile, r_where.at[h], sem.at[h]))
    for h, ref in enumerate((mine, other)):
        half = r_buf.at[pl.ds(h * AREA, AREA)]
        copies.append(pltpu.make_async_copy(ref, half, sem.at[2 + h]))
    for copy in copies:
        copy.start()
    for copy in copies[:3]:
        copy.wait()

    def look(u, count):
        for s in range(STEPS):
            for t in range(LCAP):
                i = l_where[u, 0, s * 2 * LCAP + t].astype(I32)
                k = jnp.clip(l_where[u, 0, s * 2 * LCAP + LCAP + t].astype(I32), 0, N_ROW - 1)
                dx = (me[0] + SIDE - lax.shift_right_logical(k, 3)) & (SIDE - 1)
                dy = (me[1] + SIDE - (lax.shift_right_logical(k, 1) & (SIDE - 1))) & (SIDE - 1)
                half = (me[2] + k) & 1
                place = dy * SIDE + dx
                row = r_where[half, place, 0, s * 2].astype(I32)
                j = r_where[half, place, 0, s * 2 + 1].astype(I32)
                todo[0, count] = u
                todo[1, count] = (s * LCAP + t) * BS
                todo[2, count] = half * AREA + place
                todo[3, count] = s * BS
                todo[4, count] = i * BC + j
                count = count + ((i >= 0) & (row == k)).astype(I32)
        return count

    count = lax.fori_loop(0, N_COL, look, jnp.int32(0))
    copies[3].wait()
    copies[4].wait()

    def stage(n, carry):
        rows = pl.ds(pl.multiple_of(todo[3, n], BS), BS)
        staged[n] = jnp.concatenate(split(r_buf[todo[2, n], rows, :]), axis=1)
        return carry

    lax.fori_loop(0, count, stage, 0)
    for n in range(UNROLL - 1):
        staged[count + n] = jnp.zeros(staged.shape[1:], staged.dtype)
        for field in range(5):
            todo[field, count + n] = 0
    todo[5, 0] = count


def product_kernel(todo, left, rest, staged, out_ref, l_buf, r_buf, sem, r_sem):
    steps = lax.div(todo[5, 0] + UNROLL - 1, UNROLL)

    def fetch(n):
        u, first = todo[0, n], todo[1, n]
        split_slot = first + BS > MAIN

        @pl.when(jnp.logical_not(split_slot))
        def _():
            rows = pl.ds(pl.multiple_of(first, BS), BS)
            pltpu.make_async_copy(left.at[u, rows], l_buf.at[n], sem.at[n]).start()

        @pl.when(split_slot)
        def _():
            head = pl.ds(MAIN - (BS - REST), BS - REST)
            to = l_buf.at[n, pl.ds(0, BS - REST)]
            pltpu.make_async_copy(left.at[u, head], to, sem.at[n]).start()
            to = l_buf.at[n, pl.ds(BS - REST, REST)]
            pltpu.make_async_copy(rest.at[u, pl.ds(0, REST)], to, sem.at[n]).start()

    def fetched(n):
        return pltpu.make_async_copy(left.at[0, pl.ds(0, BS)], l_buf.at[n], sem.at[n])

    def fetch_staged(step):
        some = pl.ds(step * UNROLL, UNROLL)
        return pltpu.make_async_copy(staged.at[some], r_buf.at[some], r_sem.at[step])

    def start(step, carry):
        for n in range(UNROLL):
            fetch(step * UNROLL + n)
        fetch_staged(step).start()
        return carry

    lax.fori_loop(0, steps, start, 0)
    out_ref[...] = jnp.zeros_like(out_ref)

    def multiply(step, carry):
        for n in range(UNROLL):
            fetched(step * UNROLL + n).wait()
        fetch_staged(step).wait()
        sums = []
        for n in range(UNROLL):
            at = step * UNROLL + n
            a = jnp.concatenate(split(l_buf[at]), axis=1)
            b = r_buf[at]
            both = jnp.dot(a, jnp.concatenate([b, b], axis=0), preferred_element_type=F32)
            sums.append(both[:, :BS] + both[:, BS:])
        for n in range(UNROLL):
            at = todo[4, step * UNROLL + n]
            rows = pl.ds(pl.multiple_of(lax.shift_right_logical(at, 2) * BS, BS), BS)
            cols = pl.ds(pl.multiple_of((at & (BC - 1)) * BS, BS), BS)
            out_ref[rows, cols] += sums[n]
        return carry

    lax.fori_loop(0, steps, multiply, 0)


HBM = pl.BlockSpec(memory_space=pltpu.HBM)
SMEM = pl.BlockSpec(memory_space=pltpu.SMEM)


VMEM = pl.BlockSpec(memory_space=pltpu.VMEM)
ROOM = pltpu.CompilerParams(vmem_limit_bytes=LIMIT * 1024 * 1024)


def matches(me, rest, mine, other):
    return pl.pallas_call(
        match_kernel,
        out_shape=[
            jax.ShapeDtypeStruct((6, MOST + UNROLL), I32),
            jax.ShapeDtypeStruct((MOST + UNROLL, BS, 2 * BS), jnp.bfloat16),
        ],
        in_specs=[SMEM, HBM, HBM, HBM],
        out_specs=[SMEM, VMEM],
        scratch_shapes=[
            pltpu.VMEM((2 * AREA,) + mine.shape[1:], F32),
            pltpu.SMEM((N_COL, 8, BS), F32),
            pltpu.SMEM((2, AREA, 8, BS), F32),
            pltpu.SemaphoreType.DMA((5,)),
        ],
        compiler_params=ROOM,
    )(me, rest, mine, other)


def products(todo, left, rest, staged):
    return pl.pallas_call(
        product_kernel,
        out_shape=jax.ShapeDtypeStruct((BR * BS, BC * BS), F32),
        in_specs=[SMEM, HBM, HBM, HBM],
        out_specs=VMEM,
        scratch_shapes=[
            pltpu.VMEM((MOST + UNROLL, BS, BS), F32),
            pltpu.VMEM(staged.shape, staged.dtype),
            pltpu.SemaphoreType.DMA((MOST + UNROLL,)),
            pltpu.SemaphoreType.DMA((MOST // UNROLL,)),
        ],
        compiler_params=ROOM,
    )(todo, left, rest, staged)


def per_device(left_blocks, left_index, right_blocks, right_index):
    left_blocks = left_blocks.reshape(SLOTS * BS, BS)
    left = lax.all_gather(left_blocks[:MAIN], "col", axis=0)
    mine = packed(right_blocks, right_index)
    line = jnp.stack([mine, *[along_row(mine, d, 0, 0) for d in (1, 2, 3)]])
    rest, line = lax.optimization_barrier((packed(left_blocks[MAIN:], left_index), line))
    rest = lax.all_gather(rest, "col", axis=0)
    area = jnp.concatenate([line, *[along_row(line, 0, d, 0) for d in (1, 2, 3)]])
    area, rest = lax.optimization_barrier((area, rest))
    other = along_row(area, 0, 0, 1)
    row = lax.axis_index("row")
    me = jnp.stack([row // (2 * SIDE), row // 2 % SIDE, row % 2]).astype(I32)
    todo, staged = matches(me, rest, area, other)
    return products(todo, left, rest, staged)


def solution(mesh):
    placed = (
        P(None, "row", "col", None, None),
        P(None, None, "row", "col"),
        P(None, "row", "col", None, None),
        P(None, None, "row", "col"),
    )
    return jax.shard_map(
        per_device, mesh=mesh, in_specs=placed, out_specs=P("row", "col"), check_vma=False
    )
```

```python
import jax
import jax.numpy as jnp
from jax import lax
from jax.experimental import pallas as pl
from jax.experimental.pallas import tpu as pltpu
from jax.sharding import PartitionSpec as P

BS = 128
STEPS = 2
BR = 4
BC = 4
LCAP = 2
N_ROW = 32
N_COL = 16
SIDE = 4
AREA = SIDE * SIDE
SLOTS = STEPS * LCAP
UNROLL = 4
LIMIT = 60
MOST = N_COL * SLOTS
F32 = jnp.float32
I32 = jnp.int32


def along_row(x, dx, dy, dc):
    pairs = []
    for r in range(N_ROW):
        a, b, c = r // (2 * SIDE), r // 2 % SIDE, r % 2
        to = ((a + dx) % SIDE * SIDE + (b + dy) % SIDE) * 2 + (c ^ dc)
        pairs.append((r, to))
    return lax.ppermute(x, "row", pairs)


def packed(blocks, index):
    where = index.reshape(1, -1).astype(F32)
    where = jnp.pad(where, ((0, 7), (0, BS - where.shape[1])))
    return jnp.concatenate([blocks.reshape(-1, BS), where], axis=0)


def split(x):
    high = x.astype(jnp.bfloat16)
    return high, (x - high.astype(F32)).astype(jnp.bfloat16)


def match_kernel(me, l_where, mine, other, todo, staged, r_buf, r_where, sem):
    copies = []
    for h, ref in enumerate((mine, other)):
        tile = ref.at[:, pl.ds(STEPS * BS, 8)]
        copies.append(pltpu.make_async_copy(tile, r_where.at[h], sem.at[h]))
    for h, ref in enumerate((mine, other)):
        half = r_buf.at[pl.ds(h * AREA, AREA)]
        copies.append(pltpu.make_async_copy(ref, half, sem.at[2 + h]))
    for copy in copies:
        copy.start()
    copies[0].wait()
    copies[1].wait()

    def look(u, count):
        for s in range(STEPS):
            for t in range(LCAP):
                i = l_where[u * 2 * SLOTS + s * 2 * LCAP + t]
                k = jnp.clip(l_where[u * 2 * SLOTS + s * 2 * LCAP + LCAP + t], 0, N_ROW - 1)
                dx = (me[0] + SIDE - lax.shift_right_logical(k, 3)) & (SIDE - 1)
                dy = (me[1] + SIDE - (lax.shift_right_logical(k, 1) & (SIDE - 1))) & (SIDE - 1)
                half = (me[2] + k) & 1
                place = dy * SIDE + dx
                row = r_where[half, place, 0, s * 2].astype(I32)
                j = r_where[half, place, 0, s * 2 + 1].astype(I32)
                todo[0, count] = u
                todo[1, count] = (s * LCAP + t) * BS
                todo[2, count] = half * AREA + place
                todo[3, count] = s * BS
                todo[4, count] = i * BC + j
                count = count + ((i >= 0) & (row == k)).astype(I32)
        return count

    count = lax.fori_loop(0, N_COL, look, jnp.int32(0))
    copies[2].wait()
    copies[3].wait()

    def stage(n, carry):
        rows = pl.ds(pl.multiple_of(todo[3, n], BS), BS)
        staged[n] = jnp.concatenate(split(r_buf[todo[2, n], rows, :]), axis=1)
        return carry

    lax.fori_loop(0, count, stage, 0)
    for n in range(UNROLL - 1):
        staged[count + n] = jnp.zeros(staged.shape[1:], staged.dtype)
        for field in range(5):
            todo[field, count + n] = 0
    todo[5, 0] = count


def product_kernel(todo, left, staged, product, out_ref, l_buf, r_buf, sem, r_sem, out_sem):
    steps = lax.div(todo[5, 0] + UNROLL - 1, UNROLL)

    def fetch(n):
        rows = pl.ds(pl.multiple_of(todo[1, n], BS), BS)
        return pltpu.make_async_copy(left.at[todo[0, n], rows], l_buf.at[n], sem.at[n])

    def fetch_staged(step):
        some = pl.ds(step * UNROLL, UNROLL)
        return pltpu.make_async_copy(staged.at[some], r_buf.at[some], r_sem.at[step])

    def start(step, carry):
        for n in range(UNROLL):
            fetch(step * UNROLL + n).start()
        fetch_staged(step).start()
        return carry

    lax.fori_loop(0, steps, start, 0)
    out_ref[...] = jnp.zeros_like(out_ref)

    def multiply(step, carry):
        for n in range(UNROLL):
            fetch(step * UNROLL + n).wait()
        fetch_staged(step).wait()
        sums = []
        for n in range(UNROLL):
            at = step * UNROLL + n
            a = jnp.concatenate(split(l_buf[at]), axis=1)
            b = r_buf[at]
            both = jnp.dot(a, jnp.concatenate([b, b], axis=0), preferred_element_type=F32)
            sums.append(both[:, :BS] + both[:, BS:])
        for n in range(UNROLL):
            at = todo[4, step * UNROLL + n]
            rows = pl.ds(pl.multiple_of(lax.shift_right_logical(at, 2) * BS, BS), BS)
            cols = pl.ds(pl.multiple_of((at & (BC - 1)) * BS, BS), BS)
            out_ref[rows, cols] += sums[n]
        return carry

    lax.fori_loop(0, steps, multiply, 0)
    bands = [pl.ds(i * BS, BS) for i in range(BR)]
    copies = [
        pltpu.make_async_copy(out_ref.at[band], product.at[band], out_sem.at[i])
        for i, band in enumerate(bands)
    ]
    for copy in copies:
        copy.start()
    for copy in copies:
        copy.wait()


HBM = pl.BlockSpec(memory_space=pltpu.HBM)
SMEM = pl.BlockSpec(memory_space=pltpu.SMEM)


VMEM = pl.BlockSpec(memory_space=pltpu.VMEM)
ROOM = pltpu.CompilerParams(vmem_limit_bytes=LIMIT * 1024 * 1024)


def matches(me, l_where, mine, other):
    return pl.pallas_call(
        match_kernel,
        out_shape=[
            jax.ShapeDtypeStruct((6, MOST + UNROLL), I32),
            jax.ShapeDtypeStruct((MOST + UNROLL, BS, 2 * BS), jnp.bfloat16),
        ],
        in_specs=[SMEM, SMEM, HBM, HBM],
        out_specs=[SMEM, VMEM],
        scratch_shapes=[
            pltpu.VMEM((2 * AREA,) + mine.shape[1:], F32),
            pltpu.SMEM((2, AREA, 8, BS), F32),
            pltpu.SemaphoreType.DMA((4,)),
        ],
        compiler_params=ROOM,
    )(me, l_where, mine, other)


def products(todo, left, staged):
    return pl.pallas_call(
        product_kernel,
        out_shape=jax.ShapeDtypeStruct((BR * BS, BC * BS), F32),
        in_specs=[SMEM, HBM, HBM],
        out_specs=HBM,
        scratch_shapes=[
            pltpu.VMEM((BR * BS, BC * BS), F32),
            pltpu.VMEM((MOST + UNROLL, BS, BS), F32),
            pltpu.VMEM(staged.shape, staged.dtype),
            pltpu.SemaphoreType.DMA((MOST + UNROLL,)),
            pltpu.SemaphoreType.DMA((MOST // UNROLL,)),
            pltpu.SemaphoreType.DMA((BR,)),
        ],
        compiler_params=ROOM,
    )(todo, left, staged)


def per_device(left_blocks, left_index, right_blocks, right_index):
    left = lax.all_gather(left_blocks.reshape(SLOTS * BS, BS), "col", axis=0)
    mine = packed(right_blocks, right_index)
    line = jnp.stack([mine, *[along_row(mine, d, 0, 0) for d in (1, 2, 3)]])
    l_index, line = lax.optimization_barrier((left_index, line))
    l_where = lax.all_gather(l_index.reshape(-1), "col", axis=0, tiled=True)
    area = jnp.concatenate([line, *[along_row(line, 0, d, 0) for d in (1, 2, 3)]])
    area, l_where = lax.optimization_barrier((area, l_where))
    other = along_row(area, 0, 0, 1)
    row = lax.axis_index("row")
    me = jnp.stack([row // (2 * SIDE), row // 2 % SIDE, row % 2]).astype(I32)
    todo, staged = matches(me, l_where, area, other)
    return products(todo, left, staged)


def solution(mesh):
    placed = (
        P(None, "row", "col", None, None),
        P(None, None, "row", "col"),
        P(None, "row", "col", None, None),
        P(None, None, "row", "col"),
    )
    return jax.shard_map(
        per_device, mesh=mesh, in_specs=placed, out_specs=P("row", "col"), check_vma=False
    )
```

```python
import jax
import jax.numpy as jnp
from jax import lax
from jax.experimental import pallas as pl
from jax.experimental.pallas import tpu as pltpu
from jax.sharding import PartitionSpec as P

BS = 128
STEPS = 2
BR = 4
BC = 4
LCAP = 2
N_ROW = 32
N_COL = 16
SIDE = 4
AREA = SIDE * SIDE
SLOTS = STEPS * LCAP
UNROLL = 8
LIMIT = 60
MOST = N_COL * SLOTS
F32 = jnp.float32
I32 = jnp.int32


def along_row(x, dx, dy, dc):
    pairs = []
    for r in range(N_ROW):
        a, b, c = r // (2 * SIDE), r // 2 % SIDE, r % 2
        to = ((a + dx) % SIDE * SIDE + (b + dy) % SIDE) * 2 + (c ^ dc)
        pairs.append((r, to))
    return lax.ppermute(x, "row", pairs)


def packed(blocks, index):
    where = index.reshape(1, -1).astype(F32)
    where = jnp.pad(where, ((0, 7), (0, BS - where.shape[1])))
    return jnp.concatenate([blocks.reshape(-1, BS), where], axis=0)


def split(x):
    high = x.astype(jnp.bfloat16)
    return high, (x - high.astype(F32)).astype(jnp.bfloat16)


def match_kernel(me, l_where, mine, other, todo, staged, r_buf, r_where, sem):
    copies = []
    for h, ref in enumerate((mine, other)):
        tile = ref.at[:, pl.ds(STEPS * BS, 8)]
        copies.append(pltpu.make_async_copy(tile, r_where.at[h], sem.at[h]))
    for h, ref in enumerate((mine, other)):
        half = r_buf.at[pl.ds(h * AREA, AREA)]
        copies.append(pltpu.make_async_copy(ref, half, sem.at[2 + h]))
    for copy in copies:
        copy.start()
    copies[0].wait()
    copies[1].wait()

    def look(u, count):
        for s in range(STEPS):
            for t in range(LCAP):
                i = l_where[u * 2 * SLOTS + s * 2 * LCAP + t]
                k = jnp.clip(l_where[u * 2 * SLOTS + s * 2 * LCAP + LCAP + t], 0, N_ROW - 1)
                dx = (me[0] + SIDE - lax.shift_right_logical(k, 3)) & (SIDE - 1)
                dy = (me[1] + SIDE - (lax.shift_right_logical(k, 1) & (SIDE - 1))) & (SIDE - 1)
                half = (me[2] + k) & 1
                place = dy * SIDE + dx
                row = r_where[half, place, 0, s * 2].astype(I32)
                j = r_where[half, place, 0, s * 2 + 1].astype(I32)
                todo[0, count] = u
                todo[1, count] = (s * LCAP + t) * BS
                todo[2, count] = half * AREA + place
                todo[3, count] = s * BS
                todo[4, count] = i * BC + j
                count = count + ((i >= 0) & (row == k)).astype(I32)
        return count

    count = lax.fori_loop(0, N_COL, look, jnp.int32(0))
    copies[2].wait()
    copies[3].wait()

    def stage(n, carry):
        rows = pl.ds(pl.multiple_of(todo[3, n], BS), BS)
        staged[n] = jnp.concatenate(split(r_buf[todo[2, n], rows, :]), axis=1)
        return carry

    lax.fori_loop(0, count, stage, 0)
    for n in range(UNROLL - 1):
        staged[count + n] = jnp.zeros(staged.shape[1:], staged.dtype)
        for field in range(5):
            todo[field, count + n] = 0
    todo[5, 0] = count


def product_kernel(todo, left, staged, out_ref, l_buf, r_buf, sem, r_sem):
    steps = lax.div(todo[5, 0] + UNROLL - 1, UNROLL)

    def fetch(n):
        rows = pl.ds(pl.multiple_of(todo[1, n], BS), BS)
        return pltpu.make_async_copy(left.at[todo[0, n], rows], l_buf.at[n], sem.at[n])

    def fetch_staged(step):
        some = pl.ds(step * UNROLL, UNROLL)
        return pltpu.make_async_copy(staged.at[some], r_buf.at[some], r_sem.at[step])

    def start(step, carry):
        for n in range(UNROLL):
            fetch(step * UNROLL + n).start()
        fetch_staged(step).start()
        return carry

    lax.fori_loop(0, steps, start, 0)
    out_ref[...] = jnp.zeros_like(out_ref)

    def multiply(step, carry):
        for n in range(UNROLL):
            fetch(step * UNROLL + n).wait()
        fetch_staged(step).wait()
        sums = []
        for n in range(UNROLL):
            at = step * UNROLL + n
            a = jnp.concatenate(split(l_buf[at]), axis=1)
            b = r_buf[at]
            both = jnp.dot(a, jnp.concatenate([b, b], axis=0), preferred_element_type=F32)
            sums.append(both[:, :BS] + both[:, BS:])
        for n in range(UNROLL):
            at = todo[4, step * UNROLL + n]
            rows = pl.ds(pl.multiple_of(lax.shift_right_logical(at, 2) * BS, BS), BS)
            cols = pl.ds(pl.multiple_of((at & (BC - 1)) * BS, BS), BS)
            out_ref[rows, cols] += sums[n]
        return carry

    lax.fori_loop(0, steps, multiply, 0)


HBM = pl.BlockSpec(memory_space=pltpu.HBM)
SMEM = pl.BlockSpec(memory_space=pltpu.SMEM)


VMEM = pl.BlockSpec(memory_space=pltpu.VMEM)
ROOM = pltpu.CompilerParams(vmem_limit_bytes=LIMIT * 1024 * 1024)


def matches(me, l_where, mine, other):
    return pl.pallas_call(
        match_kernel,
        out_shape=[
            jax.ShapeDtypeStruct((6, MOST + UNROLL), I32),
            jax.ShapeDtypeStruct((MOST + UNROLL, BS, 2 * BS), jnp.bfloat16),
        ],
        in_specs=[SMEM, SMEM, HBM, HBM],
        out_specs=[SMEM, VMEM],
        scratch_shapes=[
            pltpu.VMEM((2 * AREA,) + mine.shape[1:], F32),
            pltpu.SMEM((2, AREA, 8, BS), F32),
            pltpu.SemaphoreType.DMA((4,)),
        ],
        compiler_params=ROOM,
    )(me, l_where, mine, other)


def products(todo, left, staged):
    return pl.pallas_call(
        product_kernel,
        out_shape=jax.ShapeDtypeStruct((BR * BS, BC * BS), F32),
        in_specs=[SMEM, HBM, HBM],
        out_specs=VMEM,
        scratch_shapes=[
            pltpu.VMEM((MOST + UNROLL, BS, BS), F32),
            pltpu.VMEM(staged.shape, staged.dtype),
            pltpu.SemaphoreType.DMA((MOST + UNROLL,)),
            pltpu.SemaphoreType.DMA((MOST // UNROLL,)),
        ],
        compiler_params=ROOM,
    )(todo, left, staged)


def per_device(left_blocks, left_index, right_blocks, right_index):
    left = lax.all_gather(left_blocks.reshape(SLOTS * BS, BS), "col", axis=0)
    mine = packed(right_blocks, right_index)
    line = jnp.stack([mine, *[along_row(mine, d, 0, 0) for d in (1, 2, 3)]])
    l_index, line = lax.optimization_barrier((left_index, line))
    l_where = lax.all_gather(l_index.reshape(-1), "col", axis=0, tiled=True)
    area = jnp.concatenate([line, *[along_row(line, 0, d, 0) for d in (1, 2, 3)]])
    area, l_where = lax.optimization_barrier((area, l_where))
    other = along_row(area, 0, 0, 1)
    row = lax.axis_index("row")
    me = jnp.stack([row // (2 * SIDE), row // 2 % SIDE, row % 2]).astype(I32)
    todo, staged = matches(me, l_where, area, other)
    return products(todo, left, staged)


def solution(mesh):
    placed = (
        P(None, "row", "col", None, None),
        P(None, None, "row", "col"),
        P(None, "row", "col", None, None),
        P(None, None, "row", "col"),
    )
    return jax.shard_map(
        per_device, mesh=mesh, in_specs=placed, out_specs=P("row", "col"), check_vma=False
    )
```
